512 devices in a mesh: blk: 128 (over z, y, core), grp: 4 (over x).
Axes of the slice: x: 4, y: 4, z: 16, core: 2. Of those that a mesh axis runs over, the one named last changes fastest.
Arguments:
- jac_tiles: float32 [32768, 128, 128], P(('blk', 'grp')), may hold values from -0.125 to 0.125
- tile_row: int32 [32768], P(('blk', 'grp')), may hold values from 0 to 3
- tile_slot: int32 [32768], P(('blk', 'grp')), may hold values from 0 to 127, as said below
- send_list: int32 [65536], P(('blk', 'grp')), may hold values from 0 to 7
- ray_counts: int32 [2048], P(('blk', 'grp')), may hold values from 32 to 128
- travel_times: float32 [262144], P(('blk', 'grp')), may hold values from -40 to 40
Outputs:
- solution: float32 [131072], P('blk')
- ray_dir: float32 [262144], P(('blk', 'grp'))
The draws below stay inside these ranges and needn't reach their ends.
Inputs may be any that keep to these rules, and one draw needn't show every extreme that they name: `tile_slot`: the 64 tiles of one device name 64 different owners.
All inputs are finite; a program needn't handle non-finite values.
Results may differ from the reference program's by a relative error of at most 0.0003.
Values sent between devices are 32-bit elements; how exact they have to be, the bound alone decides.
A program may use at most 64 MiB of HBM per device.

```python
import math
import jax
import jax.numpy as jnp
from jax import lax

TILE = 128
RPD = 4
CPD = 8
ITERS = 2
NTD = 64
TILES = 32768
RAYS = 262144
N_BLK = 128
N_GRP = 4
DEVICES = 512


def draw_travel_times(key, part):
    key = jax.random.fold_in(key, 11)
    key_base, key_scale = jax.random.split(key)
    ray_index = jnp.arange(RAYS, dtype=jnp.float32)
    growth = jnp.exp(math.log(3.0) * ray_index / RAYS)
    base_noise = jnp.clip(jax.random.normal(key_base, (RAYS,), jnp.float32), -6.0, 6.0)
    roughness = jnp.exp(jax.random.uniform(key_scale, (RAYS,), jnp.float32, math.log(0.5), math.log(2.0)))
    return base_noise * roughness * growth


def draw_tile_slot(key, part):
    key = jax.random.fold_in(key, 23)
    device_keys = jax.random.split(key, DEVICES)
    orders = jax.vmap(lambda one_key: jax.random.permutation(one_key, N_BLK))(device_keys).astype(jnp.int32)
    relative = (orders - orders[:, :1]) % N_BLK
    position = jnp.arange(NTD, dtype=jnp.int32) % N_BLK
    device_ids = jnp.arange(DEVICES, dtype=jnp.int32)
    slots = (relative[:, position] + device_ids[:, None]) % N_BLK
    return slots.reshape(-1).astype(jnp.int32)


def touch_ends(drawn, own_key, least, largest):
    dims = drawn.shape
    place = [jax.random.randint(jax.random.fold_in(own_key, axis), (), 0, dims[axis]) for axis in range(len(dims))]
    drawn = drawn.at[tuple(place)].set(least)
    longest = dims.index(max(dims))
    place[longest] = (place[longest] + 1) % dims[longest]
    return drawn.at[tuple(place)].set(largest)


def block_levels(stream_key, extent, cuts, low, top_value):
    level = 1.0
    for dim, shards_of in cuts:
        draws = jax.random.uniform(jax.random.fold_in(jax.random.fold_in(stream_key, 6), dim), (shards_of,), jnp.float32, low / len(cuts), top_value / len(cuts))
        level = level * jnp.repeat(jnp.exp(draws), extent[dim] // shards_of).reshape((-1,) + (1,) * (len(extent) - 1 - dim))
    return level


def noise(key, shape, scale, most, pieces=(), kind=jnp.bfloat16):
    gain = block_levels(key, shape, pieces, -0.22, 0.18) if pieces else 1.0
    array = jax.random.normal(key, shape, jnp.float32) * scale * gain
    return jnp.minimum(jnp.maximum(array, -most), most).astype(kind)


def setup_inputs(seed: int = 0) -> dict:
    streams_of = jax.random.split(jax.random.key(seed), 7)
    jac_tiles = noise(streams_of[0], (TILES, TILE, TILE), (max(NTD // RPD, 1) * TILE) ** -0.5, 0.125, ((0, 512),), jnp.float32)
    tile_row = touch_ends(jax.random.randint(streams_of[1], (TILES,), 0, RPD), jax.random.fold_in(streams_of[1], 1), 0, RPD - 1).astype(jnp.int32)
    tile_slot = draw_tile_slot(jax.random.fold_in(streams_of[6], 71), 0)
    send_list = touch_ends(jax.random.randint(streams_of[3], (DEVICES * N_BLK,), 0, CPD), jax.random.fold_in(streams_of[3], 1), 0, CPD - 1).astype(jnp.int32)
    ray_counts = touch_ends(jax.random.randint(streams_of[4], (DEVICES * RPD,), TILE // 4, TILE + 1), jax.random.fold_in(streams_of[4], 1), TILE // 4, TILE).astype(jnp.int32)
    travel_times = draw_travel_times(jax.random.fold_in(streams_of[6], 71), 0)
    return {"jac_tiles": jac_tiles, "tile_row": tile_row, "tile_slot": tile_slot, "send_list": send_list, "ray_counts": ray_counts, "travel_times": travel_times}


epsilon = 1e-06

def reference(jac_tiles, tile_row, tile_slot, send_list, ray_counts, travel_times):
    devices_all = N_BLK * N_GRP
    tile_ids = jnp.arange(devices_all * NTD, dtype=jnp.int32)
    device_of = tile_ids // NTD
    blk_of = device_of // N_GRP
    grp_of = device_of % N_GRP
    row_block = device_of * RPD + tile_row
    owner_dev = tile_slot * N_GRP + grp_of
    col_block = tile_slot * CPD + send_list[owner_dev * N_BLK + blk_of]
    live_rows = (jnp.arange(TILE, dtype=jnp.int32)[None, :] < ray_counts[:, None]).astype(jnp.float32)
    highest = lax.Precision.HIGHEST

    def forward(model_dir):
        picked = model_dir[col_block]
        products = jnp.einsum('kij,kj->ki', jac_tiles, picked, precision=highest)
        summed = jax.ops.segment_sum(products, row_block, num_segments=devices_all * RPD)
        return summed * live_rows

    def transpose(ray_vec):
        spread = ray_vec[row_block]
        partial_value = jnp.einsum('kij,ki->kj', jac_tiles, spread, precision=highest)
        return jax.ops.segment_sum(partial_value, col_block, num_segments=N_BLK * CPD)
    data = travel_times.reshape(devices_all * RPD, TILE) * live_rows
    beta_norm = jnp.sqrt(jnp.sum(data * data) + epsilon)
    ray_dir = data / beta_norm
    cell_res = transpose(ray_dir)
    alpha_norm = jnp.sqrt(jnp.sum(cell_res * cell_res) + epsilon)
    model_dir = cell_res / alpha_norm
    search_dir = model_dir
    solution = jnp.zeros_like(model_dir)
    phi_bar = beta_norm
    rho_bar = alpha_norm
    for iteration in range(ITERS):
        ray_res = forward(model_dir) - alpha_norm * ray_dir
        beta_norm = jnp.sqrt(jnp.sum(ray_res * ray_res) + epsilon)
        ray_dir = ray_res / beta_norm
        cell_res = transpose(ray_dir) - beta_norm * model_dir
        alpha_norm = jnp.sqrt(jnp.sum(cell_res * cell_res) + epsilon)
        model_dir = cell_res / alpha_norm
        rho_now = jnp.sqrt(rho_bar * rho_bar + beta_norm * beta_norm)
        cosine = rho_bar / rho_now
        sine_val = beta_norm / rho_now
        theta_now = sine_val * alpha_norm
        rho_bar = -cosine * alpha_norm
        phi_now = cosine * phi_bar
        phi_bar = sine_val * phi_bar
        solution = solution + phi_now / rho_now * search_dir
        search_dir = model_dir - theta_now / rho_now * search_dir
    return (solution.reshape(-1), ray_dir.reshape(-1))
```

```python
import jax
import jax.numpy as jnp
from jax import lax
from jax.experimental import pallas as pl
from jax.experimental.pallas import tpu as pltpu
from jax.sharding import PartitionSpec as P

EPS = 1e-06
TILE = 128
NTD = 64
RPD = 4
CPD = 8
NB = 128
NG = 4
NZ = 16
NY = 8
CHUNKS = 4
MESH = pl.DeviceIdType.MESH
F32 = jnp.float32
BF16 = jnp.bfloat16


def pieces(x):
    hi = x.astype(BF16)
    rest = x - hi.astype(F32)
    mid = rest.astype(BF16)
    low = (rest - mid.astype(F32)).astype(BF16)
    return jnp.concatenate([hi, mid, low], axis=0)


def pick(onehot3, x):
    return jnp.dot(onehot3, pieces(x), preferred_element_type=F32)


def kernel(
    jac_hbm, row_hbm, slot_hbm, slotv_hbm, list_hbm, count_hbm, time_hbm,
    sol_ref, ray_ref,
    jac, row_s, slot_s, slot_v, list_v, count_s, time_v,
    ubc, live, part, state,
    send_adj, recv_adj, send_fwd, recv_fwd, send_x, recv_x,
    send_bz, recv_bz, send_bp, recv_bp, send_az, recv_az, send_ay, recv_ay,
    load_sem, small_sem, ssem, rsem,
):
    b = lax.axis_index("blk")
    g = lax.axis_index("grp")
    z, yc = b // NY, b % NY
    y, c = yc // 2, yc % 2

    per = NTD // CHUNKS
    loads = []
    for q in range(CHUNKS):
        cp = pltpu.make_async_copy(
            jac_hbm.at[q * per:(q + 1) * per], jac.at[q * per:(q + 1) * per], load_sem.at[q]
        )
        cp.start()
        loads.append(cp)
    smalls = []
    for q, (src, dst) in enumerate((
        (row_hbm, row_s), (slot_hbm, slot_s), (slotv_hbm, slot_v),
        (list_hbm, list_v), (count_hbm, count_s), (time_hbm, time_v),
    )):
        cp = pltpu.make_async_copy(src, dst, small_sem.at[q])
        cp.start()
        smalls.append(cp)

    def far_z(j):
        return (z + 8 + (1 - 2 * (j % 2)) * ((j + 1) // 2) + NZ) % NZ

    def far_blk(j):
        q = (j % NY) // 2
        yy = (y + 2 + (1 - 2 * (q % 2)) * ((q + 1) // 2) + 4) % 4
        cc = (c + 1 + j) % 2
        return far_z(j // NY) * NY + yy * 2 + cc

    def plane(j):
        i = (yc * NG + g + 1 + j) % (NY * NG)
        return i // NG, i % NG

    bar = pltpu.get_barrier_semaphore()

    def greet_blk(j, carry):
        pl.semaphore_signal(bar, inc=1, device_id=(far_blk(j), g), device_id_type=MESH)
        return carry

    def greet_grp(j, carry):
        pl.semaphore_signal(
            bar, inc=1, device_id=(z * NY + j % NY, (g + 1 + j // NY) % NG), device_id_type=MESH
        )
        return carry

    lax.fori_loop(0, NB - 1, greet_blk, 0)
    lax.fori_loop(0, NY * (NG - 1), greet_grp, 0)

    for cp in smalls:
        cp.wait()
    slot_row = slot_v[...]
    place = jnp.where(lax.broadcasted_iota(jnp.int32, (NB, NTD), 0) == slot_row, 1.0, 0.0)
    place3 = jnp.concatenate([place.astype(BF16)] * 3, axis=1)
    list_row = list_v[...]
    own = jnp.where(lax.broadcasted_iota(jnp.int32, (CPD, NB), 0) == list_row, 1.0, 0.0)
    own3 = jnp.concatenate([own.astype(BF16)] * 3, axis=1)
    serve = jnp.transpose(own)
    serve3 = jnp.concatenate([serve.astype(BF16)] * 3, axis=1)
    state[0] = jnp.zeros((TILE, TILE), F32)
    ray_index = lax.broadcasted_iota(jnp.int32, (TILE, TILE), 0)
    square = jnp.zeros((8, TILE), F32)
    for r in range(RPD):
        mask = jnp.where(ray_index < count_s[r], 1.0, 0.0)
        live[r] = mask
        d = jnp.transpose(jnp.broadcast_to(time_v[r:r + 1, :], (TILE, TILE))) * mask
        ubc[r] = d
        square = square + jnp.sum((d * d).reshape(16, 8, TILE), axis=0)

    def adjoint(lo, hi):
        def one(k, carry):
            prod = jac[k] * ubc[row_s[k]]
            part[k] = jnp.sum(prod.reshape(16, 8, TILE), axis=0)
            return carry
        lax.fori_loop(lo, hi, one, 0, unroll=4)

    def forward(vec):
        def one(k, last):
            r = row_s[k]
            prev = jnp.where(r == 0, last[0], jnp.where(r == 1, last[1], jnp.where(r == 2, last[2], last[3])))
            state[k + 1] = state[prev] + jac[k] * vec[pl.ds(slot_s[k], 1), :]
            return tuple(jnp.where(r == i, k + 1, last[i]) for i in range(RPD))
        zero = jnp.int32(0)
        last = lax.fori_loop(0, NTD, one, (zero,) * RPD, unroll=4)
        return [jnp.sum(state[last[i]], axis=1, keepdims=True) for i in range(RPD)]

    def remote(src, dst, n, device):
        pltpu.make_async_remote_copy(
            src_ref=src, dst_ref=dst, send_sem=ssem.at[n], recv_sem=rsem.at[n],
            device_id=device, device_id_type=MESH,
        ).start()

    def arrived(buf, rows, n):
        pltpu.make_async_copy(buf.at[0:rows], buf.at[0:rows], rsem.at[n]).wait()

    def left(buf, rows, n):
        pltpu.make_async_copy(buf.at[0:rows], buf.at[0:rows], ssem.at[n]).wait()

    def send_rows(src, dst, n):
        def one(j, carry):
            t = far_blk(j)
            remote(src.at[pl.ds(t, 1)], dst.at[pl.ds(b, 1)], n, (t, g))
            return carry
        lax.fori_loop(0, NB - 1, one, 0)

    def send_z(src, dst, n):
        def one(j, carry):
            remote(src.at[0:1], dst.at[pl.ds(z, 1)], n, (far_z(j) * NY + yc, g))
            return carry
        lax.fori_loop(0, NZ - 1, one, 0)

    ADJ, FWD, XCH, BZ, BP, AZ, AY = 0, 2, 4, 6, 9, 12, 14

    def beta_first(i, row):
        send_bz[i, 0:1] = row
        recv_bz[i, pl.ds(z, 1)] = row
        send_z(send_bz.at[i], recv_bz.at[i], BZ + i)

    def beta_second(i):
        arrived(recv_bz.at[i], NZ - 1, BZ + i)
        row = jnp.sum(recv_bz[i], axis=0, keepdims=True)
        send_bp[i, 0:1] = row
        recv_bp[i, pl.ds(yc * NG + g, 1)] = row

        def one(j, carry):
            q, h = plane(j)
            remote(send_bp.at[i, 0:1], recv_bp.at[i, pl.ds(yc * NG + g, 1)], BP + i, (z * NY + q, h))
            return carry
        lax.fori_loop(0, NY * NG - 1, one, 0)

    def beta_last(i):
        arrived(recv_bp.at[i], NY * NG - 1, BP + i)
        return jnp.sqrt(jnp.sum(recv_bp[i], axis=0, keepdims=True) + EPS)

    def alpha_first(i, s):
        row = jnp.sum(s * s, axis=0, keepdims=True)
        send_az[i, 0:1] = row
        recv_az[i, pl.ds(z, 1)] = row
        send_z(send_az.at[i], recv_az.at[i], AZ + i)

    def alpha_second(i):
        arrived(recv_az.at[i], NZ - 1, AZ + i)
        row = jnp.sum(recv_az[i], axis=0, keepdims=True)
        send_ay[i, 0:1] = row
        recv_ay[i, pl.ds(yc, 1)] = row

        def one(j, carry):
            q = (yc + 1 + j) % NY
            remote(send_ay.at[i, 0:1], recv_ay.at[i, pl.ds(yc, 1)], AY + i, (z * NY + q, g))
            return carry
        lax.fori_loop(0, NY - 1, one, 0)

    def alpha_last(i):
        arrived(recv_ay.at[i], NY - 1, AY + i)
        row = jnp.sum(recv_ay[i], axis=0, keepdims=True)
        total = jnp.sum(row, axis=1, keepdims=True)
        return jnp.broadcast_to(jnp.sqrt(total + EPS), (1, TILE))

    def adjoint_pack(i):
        rows = jnp.sum(part[...], axis=1)
        send_adj[i] = pick(place3, rows)

    def adjoint_send(i):
        recv_adj[i, pl.ds(b, 1)] = send_adj[i, pl.ds(b, 1)]
        send_rows(send_adj.at[i], recv_adj.at[i], ADJ + i)

    def adjoint_sum(i):
        arrived(recv_adj.at[i], NB - 1, ADJ + i)
        mine = pick(own3, recv_adj[i])
        send_x[i] = mine
        recv_x[i, pl.ds(g, 1)] = mine[None]

        def one(j, carry):
            h = (g + 1 + j) % NG
            remote(send_x.at[i], recv_x.at[i, g], XCH + i, (b, h))
            return carry
        lax.fori_loop(0, NG - 1, one, 0)

    def adjoint_total(i):
        arrived(recv_x.at[i], NG - 1, XCH + i)
        return jnp.sum(recv_x[i], axis=0)

    def forward_send(i, s):
        alpha_first(i, s)
        send_fwd[i] = pick(serve3, s)
        recv_fwd[i, pl.ds(b, 1)] = send_fwd[i, pl.ds(b, 1)]
        send_rows(send_fwd.at[i], recv_fwd.at[i], FWD + i)

    def forward_sum(i):
        alpha_second(i)
        arrived(recv_fwd.at[i], NB - 1, FWD + i)
        return forward(recv_fwd.at[i])

    def next_ray(sums, by, keep):
        total = jnp.zeros((8, TILE), F32)
        for r in range(RPD):
            t = sums[r] * live[r] * by - keep * ubc[r]
            ubc[r] = t
            total = total + jnp.sum((t * t).reshape(16, 8, TILE), axis=0)
        return jnp.sum(total, axis=0, keepdims=True)

    for q in range(CHUNKS):
        loads[q].wait()
        adjoint(q * per, (q + 1) * per)
    adjoint_pack(0)
    pl.semaphore_wait(bar, NB - 1 + NY * (NG - 1))
    beta_first(0, jnp.sum(square, axis=0, keepdims=True))
    adjoint_send(0)
    beta_second(0)
    adjoint_sum(0)
    beta0 = beta_last(0)
    s0 = adjoint_total(0) / beta0

    forward_send(0, s0)
    sums = forward_sum(0)
    alpha0 = alpha_last(0)
    square1 = next_ray(sums, 1.0 / alpha0, alpha0 / beta0)
    beta_first(1, square1)
    adjoint(0, NTD)
    adjoint_pack(1)
    adjoint_send(1)
    v0 = s0 / alpha0
    beta_second(1)
    adjoint_sum(1)
    beta1 = beta_last(1)
    s1 = adjoint_total(1) / beta1 - beta1 * v0

    forward_send(1, s1)
    rho1 = jnp.sqrt(alpha0 * alpha0 + beta1 * beta1)
    cos1, sin1 = alpha0 / rho1, beta1 / rho1
    sums = forward_sum(1)
    alpha1 = alpha_last(1)
    square2 = next_ray(sums, 1.0 / alpha1, alpha1 / beta1)
    beta_first(2, square2)
    v1 = s1 / alpha1
    theta1 = sin1 * alpha1
    rhobar = -cos1 * alpha1
    phi1 = cos1 * beta0
    phibar = sin1 * beta0
    sol = phi1 / rho1 * v0
    w1 = v1 - theta1 / rho1 * v0
    diagonal = jnp.where(ray_index == lax.broadcasted_iota(jnp.int32, (TILE, TILE), 1), 1.0, 0.0)
    rays = [jnp.sum(ubc[r] * diagonal, axis=0, keepdims=True) for r in range(RPD)]
    beta_second(2)
    beta2 = beta_last(2)
    rho2 = jnp.sqrt(rhobar * rhobar + beta2 * beta2)
    phi2 = rhobar / rho2 * phibar
    sol_ref[...] = sol + phi2 / rho2 * w1
    for r in range(RPD):
        ray_ref[r:r + 1, :] = rays[r] / beta2

    for i in range(2):
        left(send_adj.at[i], NB - 1, ADJ + i)
        left(send_fwd.at[i], NB - 1, FWD + i)
        left(recv_x.at[i], NG - 1, XCH + i)
        left(recv_az.at[i], NZ - 1, AZ + i)
        left(recv_ay.at[i], NY - 1, AY + i)
    for i in range(3):
        left(recv_bz.at[i], NZ - 1, BZ + i)
        left(recv_bp.at[i], NY * NG - 1, BP + i)


def body(jac_tiles, tile_row, tile_slot, send_list, ray_counts, travel_times):
    vmem, smem = pltpu.VMEM, pltpu.SMEM
    scratch = [
        vmem((NTD, TILE, TILE), F32), smem((NTD,), jnp.int32), smem((NTD,), jnp.int32),
        vmem((1, NTD), jnp.int32), vmem((1, NB), jnp.int32), smem((RPD,), jnp.int32),
        vmem((RPD, TILE), F32),
        vmem((RPD, TILE, TILE), F32), vmem((RPD, TILE, TILE), F32),
        vmem((NTD, 8, TILE), F32), vmem((NTD + 1, TILE, TILE), F32),
        vmem((2, NB, TILE), F32), vmem((2, NB, TILE), F32),
        vmem((2, NB, TILE), F32), vmem((2, NB, TILE), F32),
        vmem((2, CPD, TILE), F32), vmem((2, NG, CPD, TILE), F32),
        vmem((3, 8, TILE), F32), vmem((3, NZ, TILE), F32),
        vmem((3, 8, TILE), F32), vmem((3, NY * NG, TILE), F32),
        vmem((2, 8, TILE), F32), vmem((2, NZ, TILE), F32),
        vmem((2, 8, TILE), F32), vmem((2, NY, TILE), F32),
        pltpu.SemaphoreType.DMA((CHUNKS,)), pltpu.SemaphoreType.DMA((6,)),
        pltpu.SemaphoreType.DMA((16,)), pltpu.SemaphoreType.DMA((16,)),
    ]
    sol, ray = pl.pallas_call(
        kernel,
        out_shape=(
            jax.ShapeDtypeStruct((CPD, TILE), F32),
            jax.ShapeDtypeStruct((RPD, TILE), F32),
        ),
        in_specs=[pl.BlockSpec(memory_space=pl.ANY)] * 7,
        out_specs=(pl.BlockSpec(memory_space=vmem),) * 2,
        scratch_shapes=scratch,
        compiler_params=pltpu.CompilerParams(
            collective_id=0, has_side_effects=True, vmem_limit_bytes=56 * 1024 * 1024
        ),
        cost_estimate=pl.CostEstimate(flops=8 * NTD * TILE * TILE, bytes_accessed=4 * NTD * TILE * TILE, transcendentals=0),
    )(
        jac_tiles, tile_row, tile_slot, tile_slot.reshape(1, NTD), send_list.reshape(1, NB),
        ray_counts, travel_times.reshape(RPD, TILE),
    )
    return sol.reshape(-1), ray.reshape(-1)


def solution(mesh):
    spread = P(("blk", "grp"))
    in_specs = (P(("blk", "grp"), None, None),) + (spread,) * 5
    return jax.shard_map(
        body, mesh=mesh, in_specs=in_specs, out_specs=(P("blk"), spread), check_vma=False
    )
```

```python
import jax
import jax.numpy as jnp
from jax import lax
from jax.experimental import pallas as pl
from jax.experimental.pallas import tpu as pltpu
from jax.sharding import PartitionSpec as P

EPS = 1e-06
TILE = 128
NTD = 64
RPD = 4
CPD = 8
NB = 128
NG = 4
NZ = 16
NY = 8
CHUNKS = 4
MESH = pl.DeviceIdType.MESH
F32 = jnp.float32
BF16 = jnp.bfloat16


def pieces(x):
    hi = x.astype(BF16)
    rest = x - hi.astype(F32)
    mid = rest.astype(BF16)
    low = (rest - mid.astype(F32)).astype(BF16)
    return jnp.concatenate([hi, mid, low], axis=0)


def pick(onehot3, x):
    return jnp.dot(onehot3, pieces(x), preferred_element_type=F32)


def kernel(
    jac_hbm, row_hbm, slot_hbm, slotv_hbm, list_hbm, count_hbm, time_hbm,
    out_ref,
    jac, row_s, slot_s, slot_v, list_v, count_s, time_v,
    ubc, live, part, state,
    send_adj, recv_adj, send_fwd, recv_fwd, send_x, recv_x,
    send_bz, recv_bz, send_bp, recv_bp, send_az, recv_az, send_ay, recv_ay,
    load_sem, small_sem, ssem, rsem,
):
    b = lax.axis_index("blk")
    g = lax.axis_index("grp")
    z, yc = b // NY, b % NY

    per = NTD // CHUNKS
    loads = []
    for q in range(CHUNKS):
        cp = pltpu.make_async_copy(
            jac_hbm.at[q * per:(q + 1) * per], jac.at[q * per:(q + 1) * per], load_sem.at[q]
        )
        cp.start()
        loads.append(cp)
    smalls = []
    for q, (src, dst) in enumerate((
        (row_hbm, row_s), (slot_hbm, slot_s), (slotv_hbm, slot_v),
        (list_hbm, list_v), (count_hbm, count_s), (time_hbm, time_v),
    )):
        cp = pltpu.make_async_copy(src, dst, small_sem.at[q])
        cp.start()
        smalls.append(cp)

    def far_z(j):
        return (z + 8 + (1 - 2 * (j % 2)) * ((j + 1) // 2) + NZ) % NZ

    def far_blk(j):
        return far_z(j // NY) * NY + (yc + 7 * (j % NY) + 7) % NY

    def plane(j):
        i = (yc * NG + g + 1 + j) % (NY * NG)
        return i // NG, i % NG

    bar = pltpu.get_barrier_semaphore()

    def greet_blk(j, carry):
        pl.semaphore_signal(bar, inc=1, device_id=(far_blk(j), g), device_id_type=MESH)
        return carry

    def greet_grp(j, carry):
        pl.semaphore_signal(bar, inc=1, device_id=(b, (g + 1 + j) % NG), device_id_type=MESH)
        return carry

    lax.fori_loop(0, NB - 1, greet_blk, 0)
    lax.fori_loop(0, NG - 1, greet_grp, 0)

    for cp in smalls:
        cp.wait()
    slot_row = slot_v[...]
    place = jnp.where(lax.broadcasted_iota(jnp.int32, (NB, NTD), 0) == slot_row, 1.0, 0.0)
    place3 = jnp.concatenate([place.astype(BF16)] * 3, axis=1)
    list_row = list_v[...]
    own = jnp.where(lax.broadcasted_iota(jnp.int32, (CPD, NB), 0) == list_row, 1.0, 0.0)
    own3 = jnp.concatenate([own.astype(BF16)] * 3, axis=1)
    serve = jnp.transpose(own)
    serve3 = jnp.concatenate([serve.astype(BF16)] * 3, axis=1)
    state[0] = jnp.zeros((TILE, TILE), F32)
    ray_index = lax.broadcasted_iota(jnp.int32, (TILE, TILE), 0)
    square = jnp.zeros((8, TILE), F32)
    for r in range(RPD):
        mask = jnp.where(ray_index < count_s[r], 1.0, 0.0)
        live[r] = mask
        d = jnp.transpose(jnp.broadcast_to(time_v[r:r + 1, :], (TILE, TILE))) * mask
        ubc[r] = d
        square = square + jnp.sum((d * d).reshape(16, 8, TILE), axis=0)

    def adjoint(lo, hi):
        def one(k, carry):
            prod = jac[k] * ubc[row_s[k]]
            part[k] = jnp.sum(prod.reshape(16, 8, TILE), axis=0)
            return carry
        lax.fori_loop(lo, hi, one, 0, unroll=4)

    def forward(vec):
        def one(k, last):
            r = row_s[k]
            prev = jnp.where(r == 0, last[0], jnp.where(r == 1, last[1], jnp.where(r == 2, last[2], last[3])))
            state[k + 1] = state[prev] + jac[k] * vec[pl.ds(slot_s[k], 1), :]
            return tuple(jnp.where(r == i, k + 1, last[i]) for i in range(RPD))
        zero = jnp.int32(0)
        last = lax.fori_loop(0, NTD, one, (zero,) * RPD, unroll=4)
        return [jnp.sum(state[last[i]], axis=1, keepdims=True) for i in range(RPD)]

    def remote(src, dst, n, device):
        pltpu.make_async_remote_copy(
            src_ref=src, dst_ref=dst, send_sem=ssem.at[n], recv_sem=rsem.at[n],
            device_id=device, device_id_type=MESH,
        ).start()

    def arrived(buf, rows, n):
        pltpu.make_async_copy(buf.at[0:rows], buf.at[0:rows], rsem.at[n]).wait()

    def left(buf, rows, n):
        pltpu.make_async_copy(buf.at[0:rows], buf.at[0:rows], ssem.at[n]).wait()

    def send_rows(src, dst, n):
        def one(j, carry):
            t = far_blk(j)
            remote(src.at[pl.ds(t, 1)], dst.at[pl.ds(b, 1)], n, (t, g))
            return carry
        lax.fori_loop(0, NB - 1, one, 0)

    def send_z(src, dst, n):
        def one(j, carry):
            remote(src.at[0:1], dst.at[pl.ds(z, 1)], n, (far_z(j) * NY + yc, g))
            return carry
        lax.fori_loop(0, NZ - 1, one, 0)

    ADJ, FWD, XCH, BZ, BP, AZ, AY = 0, 2, 4, 6, 9, 12, 14

    def beta_first(i, row):
        send_bz[i, 0:1] = row
        recv_bz[i, pl.ds(z, 1)] = row
        send_z(send_bz.at[i], recv_bz.at[i], BZ + i)

    def beta_second(i):
        arrived(recv_bz.at[i], NZ - 1, BZ + i)
        row = jnp.sum(recv_bz[i], axis=0, keepdims=True)
        send_bp[i, 0:1] = row
        recv_bp[i, pl.ds(yc * NG + g, 1)] = row

        def one(j, carry):
            q, h = plane(j)
            remote(send_bp.at[i, 0:1], recv_bp.at[i, pl.ds(yc * NG + g, 1)], BP + i, (z * NY + q, h))
            return carry
        lax.fori_loop(0, NY * NG - 1, one, 0)

    def beta_last(i):
        arrived(recv_bp.at[i], NY * NG - 1, BP + i)
        return jnp.sqrt(jnp.sum(recv_bp[i], axis=0, keepdims=True) + EPS)

    def alpha_first(i, s):
        row = jnp.sum(s * s, axis=0, keepdims=True)
        send_az[i, 0:1] = row
        recv_az[i, pl.ds(z, 1)] = row
        send_z(send_az.at[i], recv_az.at[i], AZ + i)

    def alpha_second(i):
        arrived(recv_az.at[i], NZ - 1, AZ + i)
        row = jnp.sum(recv_az[i], axis=0, keepdims=True)
        send_ay[i, 0:1] = row
        recv_ay[i, pl.ds(yc, 1)] = row

        def one(j, carry):
            q = (yc + 1 + j) % NY
            remote(send_ay.at[i, 0:1], recv_ay.at[i, pl.ds(yc, 1)], AY + i, (z * NY + q, g))
            return carry
        lax.fori_loop(0, NY - 1, one, 0)

    def alpha_last(i):
        arrived(recv_ay.at[i], NY - 1, AY + i)
        row = jnp.sum(recv_ay[i], axis=0, keepdims=True)
        return jnp.broadcast_to(jnp.sum(row, axis=1, keepdims=True), (1, TILE))

    def adjoint_pack(i):
        rows = jnp.sum(part[...], axis=1)
        send_adj[i] = pick(place3, rows)

    def adjoint_send(i):
        recv_adj[i, pl.ds(b, 1)] = send_adj[i, pl.ds(b, 1)]
        send_rows(send_adj.at[i], recv_adj.at[i], ADJ + i)

    def adjoint_sum(i):
        arrived(recv_adj.at[i], NB - 1, ADJ + i)
        mine = pick(own3, recv_adj[i])
        send_x[i] = mine
        recv_x[i, pl.ds(g, 1)] = mine[None]

        def one(j, carry):
            h = (g + 1 + j) % NG
            remote(send_x.at[i], recv_x.at[i, g], XCH + i, (b, h))
            return carry
        lax.fori_loop(0, NG - 1, one, 0)

    def adjoint_total(i):
        arrived(recv_x.at[i], NG - 1, XCH + i)
        return jnp.sum(recv_x[i], axis=0)

    def forward_send(i, s):
        alpha_first(i, s)
        send_fwd[i] = pick(serve3, s)
        recv_fwd[i, pl.ds(b, 1)] = send_fwd[i, pl.ds(b, 1)]
        send_rows(send_fwd.at[i], recv_fwd.at[i], FWD + i)

    def forward_sum(i):
        alpha_second(i)
        arrived(recv_fwd.at[i], NB - 1, FWD + i)
        return forward(recv_fwd.at[i])

    def next_ray(sums, by, keep):
        total = jnp.zeros((8, TILE), F32)
        for r in range(RPD):
            t = sums[r] * live[r] * by - keep * ubc[r]
            ubc[r] = t
            total = total + jnp.sum((t * t).reshape(16, 8, TILE), axis=0)
        return jnp.sum(total, axis=0, keepdims=True)

    for q in range(CHUNKS):
        loads[q].wait()
        adjoint(q * per, (q + 1) * per)
    adjoint_pack(0)
    pl.semaphore_wait(bar, NB - 1 + NG - 1)
    beta_first(0, jnp.sum(square, axis=0, keepdims=True))
    adjoint_send(0)
    adjoint_sum(0)
    raw0 = adjoint_total(0)

    forward_send(0, raw0)
    beta_second(0)
    sums = forward_sum(0)
    beta0 = beta_last(0)
    alpha0 = jnp.sqrt(alpha_last(0) / (beta0 * beta0) + EPS)
    inverse = 1.0 / (alpha0 * beta0)
    square1 = next_ray(sums, inverse, alpha0 / beta0)
    beta_first(1, square1)
    adjoint(0, NTD)
    adjoint_pack(1)
    adjoint_send(1)
    v0 = raw0 * inverse
    beta_second(1)
    adjoint_sum(1)
    beta1 = beta_last(1)
    s1 = adjoint_total(1) / beta1 - beta1 * v0

    forward_send(1, s1)
    rho1 = jnp.sqrt(alpha0 * alpha0 + beta1 * beta1)
    cos1, sin1 = alpha0 / rho1, beta1 / rho1
    sums = forward_sum(1)
    alpha1 = jnp.sqrt(alpha_last(1) + EPS)
    square2 = next_ray(sums, 1.0 / alpha1, alpha1 / beta1)
    beta_first(2, square2)
    v1 = s1 / alpha1
    theta1 = sin1 * alpha1
    rhobar = -cos1 * alpha1
    phi1 = cos1 * beta0
    phibar = sin1 * beta0
    sol = phi1 / rho1 * v0
    w1 = v1 - theta1 / rho1 * v0
    diagonal = jnp.where(ray_index == lax.broadcasted_iota(jnp.int32, (TILE, TILE), 1), 1.0, 0.0)
    rays = [jnp.sum(ubc[r] * diagonal, axis=0, keepdims=True) for r in range(RPD)]
    beta_second(2)
    beta2 = beta_last(2)
    rho2 = jnp.sqrt(rhobar * rhobar + beta2 * beta2)
    phi2 = rhobar / rho2 * phibar
    out_ref[0:CPD, :] = sol + phi2 / rho2 * w1
    for r in range(RPD):
        out_ref[CPD + r:CPD + r + 1, :] = rays[r] / beta2

    for i in range(2):
        left(send_adj.at[i], NB - 1, ADJ + i)
        left(send_fwd.at[i], NB - 1, FWD + i)
        left(recv_x.at[i], NG - 1, XCH + i)
        left(recv_az.at[i], NZ - 1, AZ + i)
        left(recv_ay.at[i], NY - 1, AY + i)
    for i in range(3):
        left(recv_bz.at[i], NZ - 1, BZ + i)
        left(recv_bp.at[i], NY * NG - 1, BP + i)


def split(both_ref, sol_ref, ray_ref):
    sol_ref[...] = both_ref[:CPD]
    ray_ref[...] = both_ref[CPD:CPD + RPD]


def body(jac_tiles, tile_row, tile_slot, send_list, ray_counts, travel_times):
    vmem, smem = pltpu.VMEM, pltpu.SMEM
    scratch = [
        vmem((NTD, TILE, TILE), F32), smem((NTD,), jnp.int32), smem((NTD,), jnp.int32),
        vmem((1, NTD), jnp.int32), vmem((1, NB), jnp.int32), smem((RPD,), jnp.int32),
        vmem((RPD, TILE), F32),
        vmem((RPD, TILE, TILE), F32), vmem((RPD, TILE, TILE), F32),
        vmem((NTD, 8, TILE), F32), vmem((NTD + 1, TILE, TILE), F32),
        vmem((2, NB, TILE), F32), vmem((2, NB, TILE), F32),
        vmem((2, NB, TILE), F32), vmem((2, NB, TILE), F32),
        vmem((2, CPD, TILE), F32), vmem((2, NG, CPD, TILE), F32),
        vmem((3, 8, TILE), F32), vmem((3, NZ, TILE), F32),
        vmem((3, 8, TILE), F32), vmem((3, NY * NG, TILE), F32),
        vmem((2, 8, TILE), F32), vmem((2, NZ, TILE), F32),
        vmem((2, 8, TILE), F32), vmem((2, NY, TILE), F32),
        pltpu.SemaphoreType.DMA((CHUNKS,)), pltpu.SemaphoreType.DMA((6,)),
        pltpu.SemaphoreType.DMA((16,)), pltpu.SemaphoreType.DMA((16,)),
    ]
    both = pl.pallas_call(
        kernel,
        out_shape=jax.ShapeDtypeStruct((2 * CPD, TILE), F32),
        in_specs=[pl.BlockSpec(memory_space=pl.ANY)] * 7,
        out_specs=pl.BlockSpec(memory_space=vmem),
        scratch_shapes=scratch,
        compiler_params=pltpu.CompilerParams(
            collective_id=0, has_side_effects=True, vmem_limit_bytes=56 * 1024 * 1024
        ),
        cost_estimate=pl.CostEstimate(flops=8 * NTD * TILE * TILE, bytes_accessed=4 * NTD * TILE * TILE, transcendentals=0),
    )(
        jac_tiles, tile_row, tile_slot, tile_slot.reshape(1, NTD), send_list.reshape(1, NB),
        ray_counts, travel_times.reshape(RPD, TILE),
    )
    sol, ray = pl.pallas_call(
        split,
        out_shape=(
            jax.ShapeDtypeStruct((CPD, TILE), F32),
            jax.ShapeDtypeStruct((RPD, TILE), F32),
        ),
    )(both)
    return sol.reshape(-1), ray.reshape(-1)


def solution(mesh):
    spread = P(("blk", "grp"))
    in_specs = (P(("blk", "grp"), None, None),) + (spread,) * 5
    return jax.shard_map(
        body, mesh=mesh, in_specs=in_specs, out_specs=(P("blk"), spread), check_vma=False
    )
```

```python
import jax
import jax.numpy as jnp
from jax import lax
from jax.experimental import pallas as pl
from jax.experimental.pallas import tpu as pltpu
from jax.sharding import PartitionSpec as P

EPS = 1e-06
TILE = 128
NTD = 64
RPD = 4
CPD = 8
NB = 128
NG = 4
NZ = 16
NY = 8
CHUNKS = 4
MESH = pl.DeviceIdType.MESH
F32 = jnp.float32
BF16 = jnp.bfloat16


def pieces(x):
    hi = x.astype(BF16)
    rest = x - hi.astype(F32)
    mid = rest.astype(BF16)
    low = (rest - mid.astype(F32)).astype(BF16)
    return jnp.concatenate([hi, mid, low], axis=0)


def pick(onehot3, x):
    return jnp.dot(onehot3, pieces(x), preferred_element_type=F32)


def kernel(
    jac_hbm, row_hbm, slot_hbm, slotv_hbm, list_hbm, count_hbm, time_hbm,
    out_ref,
    jac, row_s, slot_s, slot_v, list_v, count_s, time_v,
    ubc, fbc, live, part, state,
    send_adj, recv_adj, send_fwd, recv_fwd, send_x, recv_x,
    send_bz, recv_bz, send_bp, recv_bp, send_az, recv_az, send_ay, recv_ay,
    send_end, recv_end, send_eg, recv_eg,
    load_sem, small_sem, ssem, rsem,
):
    b = lax.axis_index("blk")
    g = lax.axis_index("grp")
    z, yc = b // NY, b % NY

    def far_z(j):
        return (z + 8 + (1 - 2 * (j % 2)) * ((j + 1) // 2) + NZ) % NZ

    def far_blk(j):
        return far_z(j // NY) * NY + (yc + 7 * (j % NY) + 7) % NY

    def plane(j):
        i = (yc * NG + g + 1 + j) % (NY * NG)
        return i // NG, i % NG

    bar = pltpu.get_barrier_semaphore()

    def greet_blk(j, carry):
        pl.semaphore_signal(bar, inc=1, device_id=(far_blk(j), g), device_id_type=MESH)
        return carry

    def greet_grp(j, carry):
        pl.semaphore_signal(bar, inc=1, device_id=(b, (g + 1 + j) % NG), device_id_type=MESH)
        return carry

    lax.fori_loop(0, NB // 2, greet_blk, 0)

    per = NTD // CHUNKS
    loads = []
    for q in range(CHUNKS):
        cp = pltpu.make_async_copy(
            jac_hbm.at[q * per:(q + 1) * per], jac.at[q * per:(q + 1) * per], load_sem.at[q]
        )
        cp.start()
        loads.append(cp)
    smalls = []
    for q, (src, dst) in enumerate((
        (row_hbm, row_s), (slot_hbm, slot_s), (slotv_hbm, slot_v),
        (list_hbm, list_v), (count_hbm, count_s), (time_hbm, time_v),
    )):
        cp = pltpu.make_async_copy(src, dst, small_sem.at[q])
        cp.start()
        smalls.append(cp)

    lax.fori_loop(NB // 2, NB - 1, greet_blk, 0)
    lax.fori_loop(0, NG - 1, greet_grp, 0)

    for cp in smalls:
        cp.wait()
    slot_row = slot_v[...]
    place = jnp.where(lax.broadcasted_iota(jnp.int32, (NB, NTD), 0) == slot_row, 1.0, 0.0)
    place3 = jnp.concatenate([place.astype(BF16)] * 3, axis=1)
    list_row = list_v[...]
    own = jnp.where(lax.broadcasted_iota(jnp.int32, (CPD, NB), 0) == list_row, 1.0, 0.0)
    own3 = jnp.concatenate([own.astype(BF16)] * 3, axis=1)
    serve = jnp.transpose(own)
    serve3 = jnp.concatenate([serve.astype(BF16)] * 3, axis=1)
    state[0] = jnp.zeros((TILE, TILE), F32)
    ray_index = lax.broadcasted_iota(jnp.int32, (TILE, TILE), 0)
    square = jnp.zeros((8, TILE), F32)
    for r in range(RPD):
        mask = jnp.where(ray_index < count_s[r], 1.0, 0.0)
        live[r] = mask
        d = jnp.transpose(jnp.broadcast_to(time_v[r:r + 1, :], (TILE, TILE))) * mask
        ubc[r] = d
        square = square + jnp.sum((d * d).reshape(16, 8, TILE), axis=0)

    def adjoint(lo, hi, src):
        def one(k, carry):
            prod = jac[k] * src[row_s[k]]
            part[k] = jnp.sum(prod.reshape(16, 8, TILE), axis=0)
            return carry
        lax.fori_loop(lo, hi, one, 0, unroll=4)

    def forward(vec):
        def one(k, last):
            r = row_s[k]
            prev = jnp.where(r == 0, last[0], jnp.where(r == 1, last[1], jnp.where(r == 2, last[2], last[3])))
            state[k + 1] = state[prev] + jac[k] * vec[pl.ds(slot_s[k], 1), :]
            return tuple(jnp.where(r == i, k + 1, last[i]) for i in range(RPD))
        zero = jnp.int32(0)
        last = lax.fori_loop(0, NTD, one, (zero,) * RPD, unroll=4)
        return [jnp.sum(state[last[i]], axis=1, keepdims=True) for i in range(RPD)]

    def remote(src, dst, n, device):
        pltpu.make_async_remote_copy(
            src_ref=src, dst_ref=dst, send_sem=ssem.at[n], recv_sem=rsem.at[n],
            device_id=device, device_id_type=MESH,
        ).start()

    def arrived(buf, rows, n):
        pltpu.make_async_copy(buf.at[0:rows], buf.at[0:rows], rsem.at[n]).wait()

    def left(buf, rows, n):
        pltpu.make_async_copy(buf.at[0:rows], buf.at[0:rows], ssem.at[n]).wait()

    def send_rows(src, dst, n):
        def one(j, carry):
            t = far_blk(j)
            remote(src.at[pl.ds(t, 1)], dst.at[pl.ds(b, 1)], n, (t, g))
            return carry
        lax.fori_loop(0, NB - 1, one, 0)

    def send_z(src, dst, n):
        def one(j, carry):
            remote(src.at[0:1], dst.at[pl.ds(z, 1)], n, (far_z(j) * NY + yc, g))
            return carry
        lax.fori_loop(0, NZ - 1, one, 0)

    ADJ, FWD, XCH, BZ, BP, AZ, AY, END = 0, 2, 4, 6, 8, 10, 12, 14

    def beta_first(i, row):
        send_bz[i, 0:1] = row
        recv_bz[i, pl.ds(z, 1)] = row
        send_z(send_bz.at[i], recv_bz.at[i], BZ + i)

    def beta_second(i):
        arrived(recv_bz.at[i], NZ - 1, BZ + i)
        row = jnp.sum(recv_bz[i], axis=0, keepdims=True)
        send_bp[i, 0:1] = row
        recv_bp[i, pl.ds(yc * NG + g, 1)] = row

        def one(j, carry):
            q, h = plane(j)
            remote(send_bp.at[i, 0:1], recv_bp.at[i, pl.ds(yc * NG + g, 1)], BP + i, (z * NY + q, h))
            return carry
        lax.fori_loop(0, NY * NG - 1, one, 0)

    def beta_last(i):
        arrived(recv_bp.at[i], NY * NG - 1, BP + i)
        return jnp.sum(recv_bp[i], axis=0, keepdims=True)

    def final_first(row):
        send_end[0:1] = row
        recv_end[pl.ds(b, 1)] = row

        def one(j, carry):
            remote(send_end.at[0:1], recv_end.at[pl.ds(b, 1)], END, (far_blk(j), g))
            return carry
        lax.fori_loop(0, NB - 1, one, 0)

    def final_norm():
        arrived(recv_end, NB - 1, END)
        total = jnp.sum(recv_end[...], axis=0, keepdims=True)
        send_eg[0:1] = total
        recv_eg[pl.ds(g, 1)] = total

        def one(j, carry):
            remote(send_eg.at[0:1], recv_eg.at[pl.ds(g, 1)], END + 1, (b, (g + 1 + j) % NG))
            return carry
        lax.fori_loop(0, NG - 1, one, 0)
        arrived(recv_eg, NG - 1, END + 1)
        return jnp.sqrt(jnp.sum(recv_eg[0:NG], axis=0, keepdims=True) + EPS)

    def early_out():
        for i in range(2):
            left(send_adj.at[i], NB - 1, ADJ + i)
            left(send_fwd.at[i], NB - 1, FWD + i)
            left(recv_x.at[i], NG - 1, XCH + i)
            left(recv_az.at[i], NZ - 1, AZ + i)
            left(recv_ay.at[i], NY - 1, AY + i)
            left(recv_bz.at[i], NZ - 1, BZ + i)
            left(recv_bp.at[i], NY * NG - 1, BP + i)

    def alpha_first(i, s):
        row = jnp.sum(s * s, axis=0, keepdims=True)
        send_az[i, 0:1] = row
        recv_az[i, pl.ds(z, 1)] = row
        send_z(send_az.at[i], recv_az.at[i], AZ + i)

    def alpha_second(i):
        arrived(recv_az.at[i], NZ - 1, AZ + i)
        row = jnp.sum(recv_az[i], axis=0, keepdims=True)
        send_ay[i, 0:1] = row
        recv_ay[i, pl.ds(yc, 1)] = row

        def one(j, carry):
            q = (yc + 1 + j) % NY
            remote(send_ay.at[i, 0:1], recv_ay.at[i, pl.ds(yc, 1)], AY + i, (z * NY + q, g))
            return carry
        lax.fori_loop(0, NY - 1, one, 0)

    def alpha_last(i):
        arrived(recv_ay.at[i], NY - 1, AY + i)
        row = jnp.sum(recv_ay[i], axis=0, keepdims=True)
        return jnp.broadcast_to(jnp.sum(row, axis=1, keepdims=True), (1, TILE))

    def adjoint_pack(i):
        rows = jnp.sum(part[...], axis=1)
        send_adj[i] = pick(place3, rows)

    def adjoint_send(i):
        recv_adj[i, pl.ds(b, 1)] = send_adj[i, pl.ds(b, 1)]
        send_rows(send_adj.at[i], recv_adj.at[i], ADJ + i)

    def adjoint_sum(i):
        arrived(recv_adj.at[i], NB - 1, ADJ + i)
        mine = pick(own3, recv_adj[i])
        send_x[i] = mine
        recv_x[i, pl.ds(g, 1)] = mine[None]

        def one(j, carry):
            h = (g + 1 + j) % NG
            remote(send_x.at[i], recv_x.at[i, g], XCH + i, (b, h))
            return carry
        lax.fori_loop(0, NG - 1, one, 0)

    def adjoint_total(i):
        arrived(recv_x.at[i], NG - 1, XCH + i)
        return jnp.sum(recv_x[i], axis=0)

    def forward_send(i, s):
        alpha_first(i, s)
        send_fwd[i] = pick(serve3, s)
        recv_fwd[i, pl.ds(b, 1)] = send_fwd[i, pl.ds(b, 1)]
        send_rows(send_fwd.at[i], recv_fwd.at[i], FWD + i)

    def forward_sum(i):
        alpha_second(i)
        arrived(recv_fwd.at[i], NB - 1, FWD + i)
        return forward(recv_fwd.at[i])

    def next_ray(sums, by, keep):
        total = jnp.zeros((8, TILE), F32)
        for r in range(RPD):
            t = sums[r] * live[r] * by - keep * ubc[r]
            ubc[r] = t
            total = total + jnp.sum((t * t).reshape(16, 8, TILE), axis=0)
        return jnp.sum(total, axis=0, keepdims=True)

    for q in range(CHUNKS):
        loads[q].wait()
        adjoint(q * per, (q + 1) * per, ubc)
    adjoint_pack(0)
    pl.semaphore_wait(bar, NB - 1 + NG - 1)
    beta_first(0, jnp.sum(square, axis=0, keepdims=True))
    adjoint_send(0)
    adjoint_sum(0)
    raw0 = adjoint_total(0)

    forward_send(0, raw0)
    beta_second(0)
    sums = forward_sum(0)
    lane = lax.broadcasted_iota(jnp.int32, (1, TILE), 1)
    ff = jnp.zeros((8, TILE), F32)
    fd = jnp.zeros((8, TILE), F32)
    for r in range(RPD):
        f = sums[r] * live[r]
        fbc[r] = f
        ff = ff + jnp.sum((f * f).reshape(16, 8, TILE), axis=0)
        fd = fd + jnp.sum((f * ubc[r]).reshape(16, 8, TILE), axis=0)
    inner = jnp.where(lane < TILE // 2, jnp.sum(ff, axis=0, keepdims=True), jnp.sum(fd, axis=0, keepdims=True))
    beta_first(1, inner)
    adjoint(0, NTD, fbc)
    adjoint_pack(1)
    adjoint_send(1)
    data_square = beta_last(0)
    beta0_square = data_square + EPS
    beta0 = jnp.sqrt(beta0_square)
    alpha0 = jnp.sqrt(alpha_last(0) / beta0_square + EPS)
    inverse = 1.0 / (alpha0 * beta0)
    ratio = alpha0 / beta0
    for r in range(RPD):
        ubc[r] = fbc[r] * inverse - ratio * ubc[r]
    v0 = raw0 * inverse
    beta_second(1)
    adjoint_sum(1)
    raw1 = adjoint_total(1) * inverse - ratio * raw0
    inner = beta_last(1)
    ff = jnp.broadcast_to(jnp.sum(jnp.where(lane == 0, inner, 0.0), axis=1, keepdims=True), (1, TILE))
    fd = jnp.broadcast_to(jnp.sum(jnp.where(lane == TILE - 1, inner, 0.0), axis=1, keepdims=True), (1, TILE))
    square1 = (ff * inverse - 2.0 * ratio * fd) * inverse + ratio * ratio * data_square
    beta1 = jnp.sqrt(jnp.maximum(square1, 0.0) + EPS)
    s1 = raw1 / beta1 - beta1 * v0

    forward_send(1, s1)
    rho1 = jnp.sqrt(alpha0 * alpha0 + beta1 * beta1)
    cos1, sin1 = alpha0 / rho1, beta1 / rho1
    sums = forward_sum(1)
    alpha1 = jnp.sqrt(alpha_last(1) + EPS)
    square2 = next_ray(sums, 1.0 / alpha1, alpha1 / beta1)
    final_first(square2)
    v1 = s1 / alpha1
    theta1 = sin1 * alpha1
    rhobar = -cos1 * alpha1
    phi1 = cos1 * beta0
    phibar = sin1 * beta0
    sol = phi1 / rho1 * v0
    w1 = v1 - theta1 / rho1 * v0
    diagonal = jnp.where(ray_index == lax.broadcasted_iota(jnp.int32, (TILE, TILE), 1), 1.0, 0.0)
    rays = [jnp.sum(ubc[r] * diagonal, axis=0, keepdims=True) for r in range(RPD)]
    early_out()
    beta2 = final_norm()
    rho2 = jnp.sqrt(rhobar * rhobar + beta2 * beta2)
    phi2 = rhobar / rho2 * phibar
    out_ref[0:CPD, :] = sol + phi2 / rho2 * w1
    for r in range(RPD):
        out_ref[CPD + r:CPD + r + 1, :] = rays[r] / beta2

    left(recv_end, NB - 1, END)
    left(recv_eg, NG - 1, END + 1)


def split(both_ref, sol_ref, ray_ref):
    sol_ref[...] = both_ref[:CPD]
    ray_ref[...] = both_ref[CPD:CPD + RPD]


def body(jac_tiles, tile_row, tile_slot, send_list, ray_counts, travel_times):
    vmem, smem = pltpu.VMEM, pltpu.SMEM
    scratch = [
        vmem((NTD, TILE, TILE), F32), smem((NTD,), jnp.int32), smem((NTD,), jnp.int32),
        vmem((1, NTD), jnp.int32), vmem((1, NB), jnp.int32), smem((RPD,), jnp.int32),
        vmem((RPD, TILE), F32),
        vmem((RPD, TILE, TILE), F32), vmem((RPD, TILE, TILE), F32), vmem((RPD, TILE, TILE), F32),
        vmem((NTD, 8, TILE), F32), vmem((NTD + 1, TILE, TILE), F32),
        vmem((2, NB, TILE), F32), vmem((2, NB, TILE), F32),
        vmem((2, NB, TILE), F32), vmem((2, NB, TILE), F32),
        vmem((2, CPD, TILE), F32), vmem((2, NG, CPD, TILE), F32),
        vmem((2, 8, TILE), F32), vmem((2, NZ, TILE), F32),
        vmem((2, 8, TILE), F32), vmem((2, NY * NG, TILE), F32),
        vmem((2, 8, TILE), F32), vmem((2, NZ, TILE), F32),
        vmem((2, 8, TILE), F32), vmem((2, NY, TILE), F32),
        vmem((8, TILE), F32), vmem((NB, TILE), F32), vmem((8, TILE), F32), vmem((8, TILE), F32),
        pltpu.SemaphoreType.DMA((CHUNKS,)), pltpu.SemaphoreType.DMA((6,)),
        pltpu.SemaphoreType.DMA((16,)), pltpu.SemaphoreType.DMA((16,)),
    ]
    both = pl.pallas_call(
        kernel,
        out_shape=jax.ShapeDtypeStruct((2 * CPD, TILE), F32),
        in_specs=[pl.BlockSpec(memory_space=pl.ANY)] * 7,
        out_specs=pl.BlockSpec(memory_space=vmem),
        scratch_shapes=scratch,
        compiler_params=pltpu.CompilerParams(
            collective_id=0, has_side_effects=True, vmem_limit_bytes=56 * 1024 * 1024
        ),
        cost_estimate=pl.CostEstimate(flops=8 * NTD * TILE * TILE, bytes_accessed=4 * NTD * TILE * TILE, transcendentals=0),
    )(
        jac_tiles, tile_row, tile_slot, tile_slot.reshape(1, NTD), send_list.reshape(1, NB),
        ray_counts, travel_times.reshape(RPD, TILE),
    )
    sol, ray = pl.pallas_call(
        split,
        out_shape=(
            jax.ShapeDtypeStruct((CPD, TILE), F32),
            jax.ShapeDtypeStruct((RPD, TILE), F32),
        ),
    )(both)
    return sol.reshape(-1), ray.reshape(-1)


def solution(mesh):
    spread = P(("blk", "grp"))
    in_specs = (P(("blk", "grp"), None, None),) + (spread,) * 5
    return jax.shard_map(
        body, mesh=mesh, in_specs=in_specs, out_specs=(P("blk"), spread), check_vma=False
    )
```

```python
import jax
import jax.numpy as jnp
from jax import lax
from jax.experimental import pallas as pl
from jax.experimental.pallas import tpu as pltpu
from jax.sharding import PartitionSpec as P

EPS = 1e-06
TILE = 128
NTD = 64
RPD = 4
CPD = 8
NB = 128
NG = 4
NZ = 16
NY = 8
CHUNKS = 4
MESH = pl.DeviceIdType.MESH
F32 = jnp.float32
BF16 = jnp.bfloat16


def pieces(x):
    hi = x.astype(BF16)
    rest = x - hi.astype(F32)
    mid = rest.astype(BF16)
    low = (rest - mid.astype(F32)).astype(BF16)
    return jnp.concatenate([hi, mid, low], axis=0)


def pick(onehot3, x):
    return jnp.dot(onehot3, pieces(x), preferred_element_type=F32)


def kernel(
    jac_hbm, row_hbm, slot_hbm, slotv_hbm, list_hbm, count_hbm, time_hbm,
    out_ref,
    jac, row_s, slot_s, slot_v, list_v, count_s, time_v,
    ubc, fbc, live, part, state,
    send_adj, recv_adj, send_fwd, recv_fwd, send_x, recv_x,
    send_bz, recv_bz, send_bp, recv_bp, send_az, recv_az, send_ay, recv_ay,
    send_end, recv_end, send_eg, recv_eg,
    load_sem, small_sem, ssem, rsem,
):
    b = lax.axis_index("blk")
    g = lax.axis_index("grp")
    z, yc = b // NY, b % NY

    def far_z(j):
        return (z + 8 + (1 - 2 * (j % 2)) * ((j + 1) // 2) + NZ) % NZ

    def far_blk(j):
        return far_z(j // NY) * NY + (yc + 7 * (j % NY) + 7) % NY

    def plane(j):
        i = (yc * NG + g + 1 + j) % (NY * NG)
        return i // NG, i % NG

    bar = pltpu.get_barrier_semaphore()

    def greet_plane(k, carry):
        base = far_z(k) * NY
        for q in range(NY):
            pl.semaphore_signal(bar, inc=1, device_id=(base + q, g), device_id_type=MESH)
        return carry

    def greet_grp(j, carry):
        pl.semaphore_signal(bar, inc=1, device_id=(b, (g + 1 + j) % NG), device_id_type=MESH)
        return carry

    lax.fori_loop(0, NZ // 2, greet_plane, 0)

    per = NTD // CHUNKS
    loads = []
    for q in range(CHUNKS):
        cp = pltpu.make_async_copy(
            jac_hbm.at[q * per:(q + 1) * per], jac.at[q * per:(q + 1) * per], load_sem.at[q]
        )
        cp.start()
        loads.append(cp)
    smalls = []
    for q, (src, dst) in enumerate((
        (row_hbm, row_s), (slot_hbm, slot_s), (slotv_hbm, slot_v),
        (list_hbm, list_v), (count_hbm, count_s), (time_hbm, time_v),
    )):
        cp = pltpu.make_async_copy(src, dst, small_sem.at[q])
        cp.start()
        smalls.append(cp)

    lax.fori_loop(NZ // 2, NZ - 1, greet_plane, 0)
    for q in range(1, NY):
        pl.semaphore_signal(bar, inc=1, device_id=(z * NY + (yc + q) % NY, g), device_id_type=MESH)
    lax.fori_loop(0, NG - 1, greet_grp, 0)

    for cp in smalls:
        cp.wait()
    slot_row = slot_v[...]
    place = jnp.where(lax.broadcasted_iota(jnp.int32, (NB, NTD), 0) == slot_row, 1.0, 0.0)
    place3 = jnp.concatenate([place.astype(BF16)] * 3, axis=1)
    list_row = list_v[...]
    own = jnp.where(lax.broadcasted_iota(jnp.int32, (CPD, NB), 0) == list_row, 1.0, 0.0)
    own3 = jnp.concatenate([own.astype(BF16)] * 3, axis=1)
    serve = jnp.transpose(own)
    serve3 = jnp.concatenate([serve.astype(BF16)] * 3, axis=1)
    state[0] = jnp.zeros((TILE, TILE), F32)
    ray_index = lax.broadcasted_iota(jnp.int32, (TILE, TILE), 0)
    square = jnp.zeros((8, TILE), F32)
    for r in range(RPD):
        mask = jnp.where(ray_index < count_s[r], 1.0, 0.0)
        live[r] = mask
        d = jnp.transpose(jnp.broadcast_to(time_v[r:r + 1, :], (TILE, TILE))) * mask
        ubc[r] = d
        square = square + jnp.sum((d * d).reshape(16, 8, TILE), axis=0)

    def adjoint(lo, hi, src):
        def one(k, carry):
            prod = jac[k] * src[row_s[k]]
            part[k] = jnp.sum(prod.reshape(16, 8, TILE), axis=0)
            return carry
        lax.fori_loop(lo, hi, one, 0, unroll=16)

    def forward(vec):
        def one(k, last):
            r = row_s[k]
            prev = jnp.where(r == 0, last[0], jnp.where(r == 1, last[1], jnp.where(r == 2, last[2], last[3])))
            state[k + 1] = state[prev] + jac[k] * vec[pl.ds(slot_s[k], 1), :]
            return tuple(jnp.where(r == i, k + 1, last[i]) for i in range(RPD))
        zero = jnp.int32(0)
        last = lax.fori_loop(0, NTD, one, (zero,) * RPD, unroll=16)
        return [jnp.sum(state[last[i]], axis=1, keepdims=True) for i in range(RPD)]

    def remote(src, dst, n, device):
        pltpu.make_async_remote_copy(
            src_ref=src, dst_ref=dst, send_sem=ssem.at[n], recv_sem=rsem.at[n],
            device_id=device, device_id_type=MESH,
        ).start()

    def arrived(buf, rows, n):
        pltpu.make_async_copy(buf.at[0:rows], buf.at[0:rows], rsem.at[n]).wait()

    def left(buf, rows, n):
        pltpu.make_async_copy(buf.at[0:rows], buf.at[0:rows], ssem.at[n]).wait()

    def send_rows(src, dst, n):
        def one(j, carry):
            t = far_blk(j)
            remote(src.at[pl.ds(t, 1)], dst.at[pl.ds(b, 1)], n, (t, g))
            return carry
        lax.fori_loop(0, NB - 1, one, 0)

    def send_z(src, dst, n):
        def one(j, carry):
            remote(src.at[0:1], dst.at[pl.ds(z, 1)], n, (far_z(j) * NY + yc, g))
            return carry
        lax.fori_loop(0, NZ - 1, one, 0)

    ADJ, FWD, XCH, BZ, BP, AZ, AY, END = 0, 2, 4, 6, 8, 10, 12, 14

    def beta_first(i, row):
        send_bz[i, 0:1] = row
        recv_bz[i, pl.ds(z, 1)] = row
        send_z(send_bz.at[i], recv_bz.at[i], BZ + i)

    def beta_second(i):
        arrived(recv_bz.at[i], NZ - 1, BZ + i)
        row = jnp.sum(recv_bz[i], axis=0, keepdims=True)
        send_bp[i, 0:1] = row
        recv_bp[i, pl.ds(yc * NG + g, 1)] = row

        def one(j, carry):
            q, h = plane(j)
            remote(send_bp.at[i, 0:1], recv_bp.at[i, pl.ds(yc * NG + g, 1)], BP + i, (z * NY + q, h))
            return carry
        lax.fori_loop(0, NY * NG - 1, one, 0)

    def beta_last(i):
        arrived(recv_bp.at[i], NY * NG - 1, BP + i)
        return jnp.sum(recv_bp[i], axis=0, keepdims=True)

    def final_first(row):
        send_end[0:1] = row
        recv_end[pl.ds(b, 1)] = row

        def one(j, carry):
            remote(send_end.at[0:1], recv_end.at[pl.ds(b, 1)], END, (far_blk(j), g))
            return carry
        lax.fori_loop(0, NB - 1, one, 0)

    def final_norm():
        arrived(recv_end, NB - 1, END)
        total = jnp.sum(recv_end[...], axis=0, keepdims=True)
        send_eg[0:1] = total
        recv_eg[pl.ds(g, 1)] = total

        def one(j, carry):
            remote(send_eg.at[0:1], recv_eg.at[pl.ds(g, 1)], END + 1, (b, (g + 1 + j) % NG))
            return carry
        lax.fori_loop(0, NG - 1, one, 0)
        arrived(recv_eg, NG - 1, END + 1)
        return jnp.sum(recv_eg[0:NG], axis=0, keepdims=True)

    def early_out():
        for i in range(2):
            left(send_adj.at[i], NB - 1, ADJ + i)
            left(send_fwd.at[i], NB - 1, FWD + i)
            left(recv_x.at[i], NG - 1, XCH + i)
            left(recv_az.at[i], NZ - 1, AZ + i)
            left(recv_ay.at[i], NY - 1, AY + i)
            left(recv_bz.at[i], NZ - 1, BZ + i)
            left(recv_bp.at[i], NY * NG - 1, BP + i)

    def alpha_first(i, s):
        row = jnp.sum(s * s, axis=0, keepdims=True)
        send_az[i, 0:1] = row
        recv_az[i, pl.ds(z, 1)] = row
        send_z(send_az.at[i], recv_az.at[i], AZ + i)

    def alpha_second(i):
        arrived(recv_az.at[i], NZ - 1, AZ + i)
        row = jnp.sum(recv_az[i], axis=0, keepdims=True)
        send_ay[i, 0:1] = row
        recv_ay[i, pl.ds(yc, 1)] = row

        def one(j, carry):
            q = (yc + 1 + j) % NY
            remote(send_ay.at[i, 0:1], recv_ay.at[i, pl.ds(yc, 1)], AY + i, (z * NY + q, g))
            return carry
        lax.fori_loop(0, NY - 1, one, 0)

    def alpha_last(i):
        arrived(recv_ay.at[i], NY - 1, AY + i)
        row = jnp.sum(recv_ay[i], axis=0, keepdims=True)
        return jnp.broadcast_to(jnp.sum(row, axis=1, keepdims=True), (1, TILE))

    def adjoint_pack(i):
        rows = jnp.sum(part[...], axis=1)
        send_adj[i] = pick(place3, rows)

    def adjoint_send(i):
        recv_adj[i, pl.ds(b, 1)] = send_adj[i, pl.ds(b, 1)]
        send_rows(send_adj.at[i], recv_adj.at[i], ADJ + i)

    def adjoint_sum(i):
        arrived(recv_adj.at[i], NB - 1, ADJ + i)
        mine = pick(own3, recv_adj[i])
        send_x[i] = mine
        recv_x[i, pl.ds(g, 1)] = mine[None]

        def one(j, carry):
            h = (g + 2 + j + j // 2) % NG
            remote(send_x.at[i], recv_x.at[i, g], XCH + i, (b, h))
            return carry
        lax.fori_loop(0, NG - 1, one, 0)

    def adjoint_total(i):
        arrived(recv_x.at[i], NG - 1, XCH + i)
        return jnp.sum(recv_x[i], axis=0)

    def forward_send(i, s):
        alpha_first(i, s)
        send_fwd[i] = pick(serve3, s)
        recv_fwd[i, pl.ds(b, 1)] = send_fwd[i, pl.ds(b, 1)]
        send_rows(send_fwd.at[i], recv_fwd.at[i], FWD + i)

    def forward_sum(i):
        alpha_second(i)
        arrived(recv_fwd.at[i], NB - 1, FWD + i)
        return forward(recv_fwd.at[i])

    for q in range(CHUNKS):
        loads[q].wait()
        adjoint(q * per, (q + 1) * per, ubc)
    adjoint_pack(0)
    pl.semaphore_wait(bar, NB - 1 + NG - 1)
    adjoint_send(0)
    beta_first(0, jnp.sum(square, axis=0, keepdims=True))
    adjoint_sum(0)
    raw0 = adjoint_total(0)

    forward_send(0, raw0)
    beta_second(0)
    sums = forward_sum(0)
    lane = lax.broadcasted_iota(jnp.int32, (1, TILE), 1)
    ff = jnp.zeros((8, TILE), F32)
    fd = jnp.zeros((8, TILE), F32)
    for r in range(RPD):
        f = sums[r] * live[r]
        fbc[r] = f
        ff = ff + jnp.sum((f * f).reshape(16, 8, TILE), axis=0)
        fd = fd + jnp.sum((f * ubc[r]).reshape(16, 8, TILE), axis=0)
    inner = jnp.where(lane < TILE // 2, jnp.sum(ff, axis=0, keepdims=True), jnp.sum(fd, axis=0, keepdims=True))
    beta_first(1, inner)
    adjoint(0, NTD, fbc)
    adjoint_pack(1)
    adjoint_send(1)
    data_square = beta_last(0)
    beta0_square = data_square + EPS
    beta0 = jnp.sqrt(beta0_square)
    alpha0 = jnp.sqrt(alpha_last(0) / beta0_square + EPS)
    inverse = 1.0 / (alpha0 * beta0)
    ratio = alpha0 / beta0
    for r in range(RPD):
        ubc[r] = fbc[r] * inverse - ratio * ubc[r]
    v0 = raw0 * inverse
    beta_second(1)
    adjoint_sum(1)
    raw1 = adjoint_total(1) * inverse - ratio * raw0
    inner = beta_last(1)
    ff = jnp.broadcast_to(jnp.sum(jnp.where(lane == 0, inner, 0.0), axis=1, keepdims=True), (1, TILE))
    fd = jnp.broadcast_to(jnp.sum(jnp.where(lane == TILE - 1, inner, 0.0), axis=1, keepdims=True), (1, TILE))
    square1 = (ff * inverse - 2.0 * ratio * fd) * inverse + ratio * ratio * data_square
    beta1 = jnp.sqrt(jnp.maximum(square1, 0.0) + EPS)
    s1 = raw1 / beta1 - beta1 * v0

    forward_send(1, s1)
    rho1 = jnp.sqrt(alpha0 * alpha0 + beta1 * beta1)
    cos1, sin1 = alpha0 / rho1, beta1 / rho1
    sums = forward_sum(1)
    gg = jnp.zeros((8, TILE), F32)
    gt = jnp.zeros((8, TILE), F32)
    tt = jnp.zeros((8, TILE), F32)
    for r in range(RPD):
        f = sums[r] * live[r]
        t = ubc[r]
        fbc[r] = f
        gg = gg + jnp.sum((f * f).reshape(16, 8, TILE), axis=0)
        gt = gt + jnp.sum((f * t).reshape(16, 8, TILE), axis=0)
        tt = tt + jnp.sum((t * t).reshape(16, 8, TILE), axis=0)
    gg, gt, tt = (jnp.sum(v, axis=0, keepdims=True) for v in (gg, gt, tt))
    final_first(jnp.where(lane < 32, gg, jnp.where(lane < 64, gt, tt)))
    alpha1 = jnp.sqrt(alpha_last(1) + EPS)
    v1 = s1 / alpha1
    theta1 = sin1 * alpha1
    rhobar = -cos1 * alpha1
    phi1 = cos1 * beta0
    phibar = sin1 * beta0
    sol = phi1 / rho1 * v0
    w1 = v1 - theta1 / rho1 * v0
    step = alpha1 / beta1
    diagonal = jnp.where(ray_index == lax.broadcasted_iota(jnp.int32, (TILE, TILE), 1), 1.0, 0.0)
    rays = [
        jnp.sum((fbc[r] / alpha1 - step * ubc[r]) * diagonal, axis=0, keepdims=True) for r in range(RPD)
    ]
    early_out()
    inner = final_norm()
    gg, gt, tt = (
        jnp.broadcast_to(jnp.sum(jnp.where(lane == at, inner, 0.0), axis=1, keepdims=True), (1, TILE))
        for at in (0, 32, 64)
    )
    square2 = (gg / alpha1 - 2.0 * step * gt) / alpha1 + step * step * tt
    beta2 = jnp.sqrt(jnp.maximum(square2, 0.0) + EPS)
    rho2 = jnp.sqrt(rhobar * rhobar + beta2 * beta2)
    phi2 = rhobar / rho2 * phibar
    out_ref[0:CPD, :] = sol + phi2 / rho2 * w1
    for r in range(RPD):
        out_ref[CPD + r:CPD + r + 1, :] = rays[r] / beta2

    left(recv_end, NB - 1, END)
    left(recv_eg, NG - 1, END + 1)


def split(both_ref, sol_ref, ray_ref):
    sol_ref[...] = both_ref[:CPD]
    ray_ref[...] = both_ref[CPD:CPD + RPD]


def body(jac_tiles, tile_row, tile_slot, send_list, ray_counts, travel_times):
    vmem, smem = pltpu.VMEM, pltpu.SMEM
    scratch = [
        vmem((NTD, TILE, TILE), F32), smem((NTD,), jnp.int32), smem((NTD,), jnp.int32),
        vmem((1, NTD), jnp.int32), vmem((1, NB), jnp.int32), smem((RPD,), jnp.int32),
        vmem((RPD, TILE), F32),
        vmem((RPD, TILE, TILE), F32), vmem((RPD, TILE, TILE), F32), vmem((RPD, TILE, TILE), F32),
        vmem((NTD, 8, TILE), F32), vmem((NTD + 1, TILE, TILE), F32),
        vmem((2, NB, TILE), F32), vmem((2, NB, TILE), F32),
        vmem((2, NB, TILE), F32), vmem((2, NB, TILE), F32),
        vmem((2, CPD, TILE), F32), vmem((2, NG, CPD, TILE), F32),
        vmem((2, 8, TILE), F32), vmem((2, NZ, TILE), F32),
        vmem((2, 8, TILE), F32), vmem((2, NY * NG, TILE), F32),
        vmem((2, 8, TILE), F32), vmem((2, NZ, TILE), F32),
        vmem((2, 8, TILE), F32), vmem((2, NY, TILE), F32),
        vmem((8, TILE), F32), vmem((NB, TILE), F32), vmem((8, TILE), F32), vmem((8, TILE), F32),
        pltpu.SemaphoreType.DMA((CHUNKS,)), pltpu.SemaphoreType.DMA((6,)),
        pltpu.SemaphoreType.DMA((16,)), pltpu.SemaphoreType.DMA((16,)),
    ]
    both = pl.pallas_call(
        kernel,
        out_shape=jax.ShapeDtypeStruct((2 * CPD, TILE), F32),
        in_specs=[pl.BlockSpec(memory_space=pl.ANY)] * 7,
        out_specs=pl.BlockSpec(memory_space=vmem),
        scratch_shapes=scratch,
        compiler_params=pltpu.CompilerParams(
            collective_id=0, has_side_effects=True, vmem_limit_bytes=56 * 1024 * 1024
        ),
        cost_estimate=pl.CostEstimate(flops=8 * NTD * TILE * TILE, bytes_accessed=4 * NTD * TILE * TILE, transcendentals=0),
    )(
        jac_tiles, tile_row, tile_slot, tile_slot.reshape(1, NTD), send_list.reshape(1, NB),
        ray_counts, travel_times.reshape(RPD, TILE),
    )
    sol, ray = pl.pallas_call(
        split,
        out_shape=(
            jax.ShapeDtypeStruct((CPD, TILE), F32),
            jax.ShapeDtypeStruct((RPD, TILE), F32),
        ),
    )(both)
    return sol.reshape(-1), ray.reshape(-1)


def solution(mesh):
    spread = P(("blk", "grp"))
    in_specs = (P(("blk", "grp"), None, None),) + (spread,) * 5
    return jax.shard_map(
        body, mesh=mesh, in_specs=in_specs, out_specs=(P("blk"), spread), check_vma=False
    )
```

```python
import jax
import jax.numpy as jnp
from jax import lax
from jax.experimental import pallas as pl
from jax.experimental.pallas import tpu as pltpu
from jax.sharding import PartitionSpec as P

EPS = 1e-06
TILE = 128
NTD = 64
RPD = 4
CPD = 8
NB = 128
NG = 4
NZ = 16
NY = 8
CHUNKS = 4
MESH = pl.DeviceIdType.MESH
F32 = jnp.float32
BF16 = jnp.bfloat16


def pieces(x):
    hi = x.astype(BF16)
    rest = x - hi.astype(F32)
    mid = rest.astype(BF16)
    low = (rest - mid.astype(F32)).astype(BF16)
    return jnp.concatenate([hi, mid, low], axis=0)


def pick(onehot3, x):
    return jnp.dot(onehot3, pieces(x), preferred_element_type=F32)


def kernel(
    jac_hbm, row_hbm, slot_hbm, slotv_hbm, list_hbm, count_hbm, time_hbm,
    out_ref,
    jac, row_s, slot_s, slot_v, list_v, count_s, time_v,
    ubc, fbc, live, part, state,
    send_adj, recv_adj, send_fwd, recv_fwd, send_x, recv_x,
    send_bz, recv_bz, send_bp, recv_bp, send_az, recv_az, send_ay, recv_ay,
    send_end, recv_end, send_eg, recv_eg,
    load_sem, small_sem, ssem, rsem,
):
    b = lax.axis_index("blk")
    g = lax.axis_index("grp")
    z, yc = b // NY, b % NY

    def far_z(j):
        return (z + 8 + (1 - 2 * (j % 2)) * ((j + 1) // 2) + NZ) % NZ

    def far_blk(j):
        return far_z(j // NY) * NY + (yc + 7 * (j % NY) + 7) % NY

    def plane(j):
        i = (yc * NG + g + 1 + j) % (NY * NG)
        return i // NG, i % NG

    bar = pltpu.get_barrier_semaphore()

    def greet_plane(k, carry):
        base = far_z(k) * NY
        for q in range(NY):
            pl.semaphore_signal(bar, inc=1, device_id=(base + q, g), device_id_type=MESH)
        return carry

    def greet_grp(j, carry):
        pl.semaphore_signal(bar, inc=1, device_id=(b, (g + 1 + j) % NG), device_id_type=MESH)
        return carry

    lax.fori_loop(0, NZ // 2, greet_plane, 0)

    per = NTD // CHUNKS
    loads = []
    for q in range(CHUNKS):
        cp = pltpu.make_async_copy(
            jac_hbm.at[q * per:(q + 1) * per], jac.at[q * per:(q + 1) * per], load_sem.at[q]
        )
        cp.start()
        loads.append(cp)
    smalls = []
    for q, (src, dst) in enumerate((
        (row_hbm, row_s), (slot_hbm, slot_s), (slotv_hbm, slot_v),
        (list_hbm, list_v), (count_hbm, count_s), (time_hbm, time_v),
    )):
        cp = pltpu.make_async_copy(src, dst, small_sem.at[q])
        cp.start()
        smalls.append(cp)

    lax.fori_loop(NZ // 2, NZ - 1, greet_plane, 0)
    for q in range(1, NY):
        pl.semaphore_signal(bar, inc=1, device_id=(z * NY + (yc + q) % NY, g), device_id_type=MESH)
    lax.fori_loop(0, NG - 1, greet_grp, 0)

    for cp in smalls:
        cp.wait()
    slot_row = slot_v[...]
    place = jnp.where(lax.broadcasted_iota(jnp.int32, (NB, NTD), 0) == slot_row, 1.0, 0.0)
    place3 = jnp.concatenate([place.astype(BF16)] * 3, axis=1)
    list_row = list_v[...]
    own = jnp.where(lax.broadcasted_iota(jnp.int32, (CPD, NB), 0) == list_row, 1.0, 0.0)
    own3 = jnp.concatenate([own.astype(BF16)] * 3, axis=1)
    serve = jnp.transpose(own)
    serve3 = jnp.concatenate([serve.astype(BF16)] * 3, axis=1)
    state[0] = jnp.zeros((TILE, TILE), F32)
    ray_index = lax.broadcasted_iota(jnp.int32, (TILE, TILE), 0)
    square = jnp.zeros((8, TILE), F32)
    for r in range(RPD):
        mask = jnp.where(ray_index < count_s[r], 1.0, 0.0)
        live[r] = mask
        d = jnp.transpose(jnp.broadcast_to(time_v[r:r + 1, :], (TILE, TILE))) * mask
        ubc[r] = d
        square = square + jnp.sum((d * d).reshape(16, 8, TILE), axis=0)

    def adjoint(lo, hi, src):
        def one(k, carry):
            prod = jac[k] * src[row_s[k]]
            part[k] = jnp.sum(prod.reshape(16, 8, TILE), axis=0)
            return carry
        lax.fori_loop(lo, hi, one, 0, unroll=32)

    def forward(vec):
        def one(k, last):
            r = row_s[k]
            prev = jnp.where(r == 0, last[0], jnp.where(r == 1, last[1], jnp.where(r == 2, last[2], last[3])))
            state[k + 1] = state[prev] + jac[k] * vec[pl.ds(slot_s[k], 1), :]
            return tuple(jnp.where(r == i, k + 1, last[i]) for i in range(RPD))
        zero = jnp.int32(0)
        last = lax.fori_loop(0, NTD, one, (zero,) * RPD, unroll=32)
        return [jnp.sum(state[last[i]], axis=1, keepdims=True) for i in range(RPD)]

    def remote(src, dst, n, device):
        pltpu.make_async_remote_copy(
            src_ref=src, dst_ref=dst, send_sem=ssem.at[n], recv_sem=rsem.at[n],
            device_id=device, device_id_type=MESH,
        ).start()

    def arrived(buf, rows, n):
        pltpu.make_async_copy(buf.at[0:rows], buf.at[0:rows], rsem.at[n]).wait()

    def left(buf, rows, n):
        pltpu.make_async_copy(buf.at[0:rows], buf.at[0:rows], ssem.at[n]).wait()

    def send_rows(src, dst, n):
        def one(j, carry):
            t = far_blk(j)
            remote(src.at[pl.ds(t, 1)], dst.at[pl.ds(b, 1)], n, (t, g))
            return carry
        lax.fori_loop(0, NB - 1, one, 0)

    def send_z(src, dst, n):
        def one(j, carry):
            remote(src.at[0:1], dst.at[pl.ds(z, 1)], n, (far_z(j) * NY + yc, g))
            return carry
        lax.fori_loop(0, NZ - 1, one, 0)

    ADJ, FWD, XCH, BZ, BP, AZ, AY, END = 0, 2, 4, 6, 8, 10, 12, 14

    def beta_first(i, row):
        send_bz[i, 0:1] = row
        recv_bz[i, pl.ds(z, 1)] = row
        send_z(send_bz.at[i], recv_bz.at[i], BZ + i)

    def beta_second(i):
        arrived(recv_bz.at[i], NZ - 1, BZ + i)
        row = jnp.sum(recv_bz[i], axis=0, keepdims=True)
        send_bp[i, 0:1] = row
        recv_bp[i, pl.ds(yc * NG + g, 1)] = row

        def one(j, carry):
            q, h = plane(j)
            remote(send_bp.at[i, 0:1], recv_bp.at[i, pl.ds(yc * NG + g, 1)], BP + i, (z * NY + q, h))
            return carry
        lax.fori_loop(0, NY * NG - 1, one, 0)

    def beta_last(i):
        arrived(recv_bp.at[i], NY * NG - 1, BP + i)
        return jnp.sum(recv_bp[i], axis=0, keepdims=True)

    def final_first(row):
        send_end[0:1] = row
        recv_end[pl.ds(b, 1)] = row

        def one(j, carry):
            remote(send_end.at[0:1], recv_end.at[pl.ds(b, 1)], END, (far_blk(j), g))
            return carry
        lax.fori_loop(0, NB - 1, one, 0)

    def final_norm():
        arrived(recv_end, NB - 1, END)
        total = jnp.sum(recv_end[...], axis=0, keepdims=True)
        send_eg[0:1] = total
        recv_eg[pl.ds(g, 1)] = total

        def one(j, carry):
            remote(send_eg.at[0:1], recv_eg.at[pl.ds(g, 1)], END + 1, (b, (g + 2 + j + j // 2) % NG))
            return carry
        lax.fori_loop(0, NG - 1, one, 0)
        arrived(recv_eg, NG - 1, END + 1)
        return jnp.sum(recv_eg[0:NG], axis=0, keepdims=True)

    def early_out():
        for i in range(2):
            left(send_adj.at[i], NB - 1, ADJ + i)
            left(send_fwd.at[i], NB - 1, FWD + i)
            left(recv_x.at[i], NG - 1, XCH + i)
            left(recv_az.at[i], NZ - 1, AZ + i)
            left(recv_ay.at[i], NY - 1, AY + i)
            left(recv_bz.at[i], NZ - 1, BZ + i)
            left(recv_bp.at[i], NY * NG - 1, BP + i)

    def alpha_first(i, s):
        row = jnp.sum(s * s, axis=0, keepdims=True)
        send_az[i, 0:1] = row
        recv_az[i, pl.ds(z, 1)] = row
        send_z(send_az.at[i], recv_az.at[i], AZ + i)

    def alpha_second(i):
        arrived(recv_az.at[i], NZ - 1, AZ + i)
        row = jnp.sum(recv_az[i], axis=0, keepdims=True)
        send_ay[i, 0:1] = row
        recv_ay[i, pl.ds(yc, 1)] = row

        def one(j, carry):
            q = (yc + 1 + j) % NY
            remote(send_ay.at[i, 0:1], recv_ay.at[i, pl.ds(yc, 1)], AY + i, (z * NY + q, g))
            return carry
        lax.fori_loop(0, NY - 1, one, 0)

    def alpha_last(i):
        arrived(recv_ay.at[i], NY - 1, AY + i)
        row = jnp.sum(recv_ay[i], axis=0, keepdims=True)
        return jnp.broadcast_to(jnp.sum(row, axis=1, keepdims=True), (1, TILE))

    def adjoint_pack(i):
        rows = jnp.sum(part[...], axis=1)
        send_adj[i] = pick(place3, rows)

    def adjoint_send(i):
        recv_adj[i, pl.ds(b, 1)] = send_adj[i, pl.ds(b, 1)]
        send_rows(send_adj.at[i], recv_adj.at[i], ADJ + i)

    def adjoint_sum(i):
        arrived(recv_adj.at[i], NB - 1, ADJ + i)
        mine = pick(own3, recv_adj[i])
        send_x[i] = mine
        recv_x[i, pl.ds(g, 1)] = mine[None]

        def one(j, carry):
            h = (g + 2 + j + j // 2) % NG
            remote(send_x.at[i], recv_x.at[i, g], XCH + i, (b, h))
            return carry
        lax.fori_loop(0, NG - 1, one, 0)

    def adjoint_total(i):
        arrived(recv_x.at[i], NG - 1, XCH + i)
        return jnp.sum(recv_x[i], axis=0)

    def forward_send(i, s):
        alpha_first(i, s)
        send_fwd[i] = pick(serve3, s)
        recv_fwd[i, pl.ds(b, 1)] = send_fwd[i, pl.ds(b, 1)]
        send_rows(send_fwd.at[i], recv_fwd.at[i], FWD + i)

    def forward_sum(i):
        alpha_second(i)
        arrived(recv_fwd.at[i], NB - 1, FWD + i)
        return forward(recv_fwd.at[i])

    for q in range(CHUNKS):
        loads[q].wait()
        adjoint(q * per, (q + 1) * per, ubc)
    adjoint_pack(0)
    pl.semaphore_wait(bar, NB - 1 + NG - 1)
    adjoint_send(0)
    beta_first(0, jnp.sum(square, axis=0, keepdims=True))
    adjoint_sum(0)
    raw0 = adjoint_total(0)

    forward_send(0, raw0)
    beta_second(0)
    sums = forward_sum(0)
    lane = lax.broadcasted_iota(jnp.int32, (1, TILE), 1)
    ff = jnp.zeros((8, TILE), F32)
    fd = jnp.zeros((8, TILE), F32)
    for r in range(RPD):
        f = sums[r] * live[r]
        fbc[r] = f
        ff = ff + jnp.sum((f * f).reshape(16, 8, TILE), axis=0)
        fd = fd + jnp.sum((f * ubc[r]).reshape(16, 8, TILE), axis=0)
    inner = jnp.where(lane < TILE // 2, jnp.sum(ff, axis=0, keepdims=True), jnp.sum(fd, axis=0, keepdims=True))
    beta_first(1, inner)
    adjoint(0, NTD, fbc)
    adjoint_pack(1)
    adjoint_send(1)
    data_square = beta_last(0)
    beta0_square = data_square + EPS
    beta0 = jnp.sqrt(beta0_square)
    alpha0 = jnp.sqrt(alpha_last(0) / beta0_square + EPS)
    inverse = 1.0 / (alpha0 * beta0)
    ratio = alpha0 / beta0
    for r in range(RPD):
        ubc[r] = fbc[r] * inverse - ratio * ubc[r]
    v0 = raw0 * inverse
    beta_second(1)
    adjoint_sum(1)
    raw1 = adjoint_total(1) * inverse - ratio * raw0
    inner = beta_last(1)
    ff = jnp.broadcast_to(jnp.sum(jnp.where(lane == 0, inner, 0.0), axis=1, keepdims=True), (1, TILE))
    fd = jnp.broadcast_to(jnp.sum(jnp.where(lane == TILE - 1, inner, 0.0), axis=1, keepdims=True), (1, TILE))
    square1 = (ff * inverse - 2.0 * ratio * fd) * inverse + ratio * ratio * data_square
    beta1 = jnp.sqrt(jnp.maximum(square1, 0.0) + EPS)
    s1 = raw1 / beta1 - beta1 * v0

    forward_send(1, s1)
    rho1 = jnp.sqrt(alpha0 * alpha0 + beta1 * beta1)
    cos1, sin1 = alpha0 / rho1, beta1 / rho1
    sums = forward_sum(1)
    gg = jnp.zeros((8, TILE), F32)
    gt = jnp.zeros((8, TILE), F32)
    tt = jnp.zeros((8, TILE), F32)
    for r in range(RPD):
        f = sums[r] * live[r]
        t = ubc[r]
        fbc[r] = f
        gg = gg + jnp.sum((f * f).reshape(16, 8, TILE), axis=0)
        gt = gt + jnp.sum((f * t).reshape(16, 8, TILE), axis=0)
        tt = tt + jnp.sum((t * t).reshape(16, 8, TILE), axis=0)
    gg, gt, tt = (jnp.sum(v, axis=0, keepdims=True) for v in (gg, gt, tt))
    final_first(jnp.where(lane < 32, gg, jnp.where(lane < 64, gt, tt)))
    alpha1 = jnp.sqrt(alpha_last(1) + EPS)
    v1 = s1 / alpha1
    theta1 = sin1 * alpha1
    rhobar = -cos1 * alpha1
    phi1 = cos1 * beta0
    phibar = sin1 * beta0
    sol = phi1 / rho1 * v0
    w1 = v1 - theta1 / rho1 * v0
    step = alpha1 / beta1
    diagonal = jnp.where(ray_index == lax.broadcasted_iota(jnp.int32, (TILE, TILE), 1), 1.0, 0.0)
    rays = [
        jnp.sum((fbc[r] / alpha1 - step * ubc[r]) * diagonal, axis=0, keepdims=True) for r in range(RPD)
    ]
    early_out()
    inner = final_norm()
    gg, gt, tt = (
        jnp.broadcast_to(jnp.sum(jnp.where(lane == at, inner, 0.0), axis=1, keepdims=True), (1, TILE))
        for at in (0, 32, 64)
    )
    square2 = (gg / alpha1 - 2.0 * step * gt) / alpha1 + step * step * tt
    beta2 = jnp.sqrt(jnp.maximum(square2, 0.0) + EPS)
    rho2 = jnp.sqrt(rhobar * rhobar + beta2 * beta2)
    phi2 = rhobar / rho2 * phibar
    out_ref[0:CPD, :] = sol + phi2 / rho2 * w1
    for r in range(RPD):
        out_ref[CPD + r:CPD + r + 1, :] = rays[r] / beta2

    left(recv_end, NB - 1, END)
    left(recv_eg, NG - 1, END + 1)


def split(both_ref, sol_ref, ray_ref):
    sol_ref[...] = both_ref[:CPD]
    ray_ref[...] = both_ref[CPD:CPD + RPD]


def body(jac_tiles, tile_row, tile_slot, send_list, ray_counts, travel_times):
    vmem, smem = pltpu.VMEM, pltpu.SMEM
    scratch = [
        vmem((NTD, TILE, TILE), F32), smem((NTD,), jnp.int32), smem((NTD,), jnp.int32),
        vmem((1, NTD), jnp.int32), vmem((1, NB), jnp.int32), smem((RPD,), jnp.int32),
        vmem((RPD, TILE), F32),
        vmem((RPD, TILE, TILE), F32), vmem((RPD, TILE, TILE), F32), vmem((RPD, TILE, TILE), F32),
        vmem((NTD, 8, TILE), F32), vmem((NTD + 1, TILE, TILE), F32),
        vmem((2, NB, TILE), F32), vmem((2, NB, TILE), F32),
        vmem((2, NB, TILE), F32), vmem((2, NB, TILE), F32),
        vmem((2, CPD, TILE), F32), vmem((2, NG, CPD, TILE), F32),
        vmem((2, 8, TILE), F32), vmem((2, NZ, TILE), F32),
        vmem((2, 8, TILE), F32), vmem((2, NY * NG, TILE), F32),
        vmem((2, 8, TILE), F32), vmem((2, NZ, TILE), F32),
        vmem((2, 8, TILE), F32), vmem((2, NY, TILE), F32),
        vmem((8, TILE), F32), vmem((NB, TILE), F32), vmem((8, TILE), F32), vmem((8, TILE), F32),
        pltpu.SemaphoreType.DMA((CHUNKS,)), pltpu.SemaphoreType.DMA((6,)),
        pltpu.SemaphoreType.DMA((16,)), pltpu.SemaphoreType.DMA((16,)),
    ]
    both = pl.pallas_call(
        kernel,
        out_shape=jax.ShapeDtypeStruct((2 * CPD, TILE), F32),
        in_specs=[pl.BlockSpec(memory_space=pl.ANY)] * 7,
        out_specs=pl.BlockSpec(memory_space=vmem),
        scratch_shapes=scratch,
        compiler_params=pltpu.CompilerParams(
            collective_id=0, has_side_effects=True, vmem_limit_bytes=56 * 1024 * 1024
        ),
        cost_estimate=pl.CostEstimate(flops=8 * NTD * TILE * TILE, bytes_accessed=4 * NTD * TILE * TILE, transcendentals=0),
    )(
        jac_tiles, tile_row, tile_slot, tile_slot.reshape(1, NTD), send_list.reshape(1, NB),
        ray_counts, travel_times.reshape(RPD, TILE),
    )
    sol, ray = pl.pallas_call(
        split,
        out_shape=(
            jax.ShapeDtypeStruct((CPD, TILE), F32),
            jax.ShapeDtypeStruct((RPD, TILE), F32),
        ),
    )(both)
    return sol.reshape(-1), ray.reshape(-1)


def solution(mesh):
    spread = P(("blk", "grp"))
    in_specs = (P(("blk", "grp"), None, None),) + (spread,) * 5
    return jax.shard_map(
        body, mesh=mesh, in_specs=in_specs, out_specs=(P("blk"), spread), check_vma=False
    )
```
